128 devices in a mesh: fsdp: 16 (over z, y), grp: 8 (over x, core).
Axes of the slice: x: 4, y: 4, z: 4, core: 2. Of those that a mesh axis runs over, the one named last changes fastest.
Arguments:
- tokens: bfloat16 [16384, 4096], P('fsdp'), may hold values from -6 to 6
- database: bfloat16 [128, 128, 896], P('fsdp'), may hold values from -6 to 6
- neighbour_ids: int32 [256, 2], P('fsdp'), may hold values from 0 to 127, as said below
- shard_map: int32 [128], replicated, may hold values from 0 to 127, as said below
- q_weight: bfloat16 [4096, 4096], P('fsdp', 'grp'), may hold values from -0.09375 to 0.09375
- k_weight: bfloat16 [896, 4096], P('fsdp', 'grp'), may hold values from -0.1875 to 0.1875
- v_weight: bfloat16 [896, 4096], P('fsdp', 'grp'), may hold values from -0.1875 to 0.1875
- o_weight: bfloat16 [4096, 4096], P('grp', 'fsdp'), may hold values from -0.75 to 0.75
Outputs:
- mixed: bfloat16 [16384, 4096], P(('fsdp', 'grp'))
The draws below stay inside these ranges and needn't reach their ends.
Inputs may be any that keep to these rules, and one draw needn't show every extreme that they name: shard_map is a permutation: database span id i lies on index shard_map[i] // 8 of fsdp, as its local span shard_map[i] % 8. `neighbour_ids`: among the 32 neighbour ids of the spans of one index of fsdp, at most 4 lie on any one index of fsdp; in every draw one index of fsdp holds exactly 4 of them for every index's spans. Ids may repeat.
All inputs are finite; a program needn't handle non-finite values.
Results may differ from the reference program's by a relative error of at most 0.018.
Values may be sent and summed in bfloat16 or wider, within the bound.
No kernel may reach another device: no remote copies, remote signals or barrier semaphores. Data moves between devices by JAX's collectives and lax.ppermute only.
A program may use at most 128 MiB of HBM per device.

```python
import math
import jax
import jax.numpy as jnp
from jax import lax

D = 4096
HEADS = 32
HEAD = 128
ENC = 896
SPAN = 64
NLEN = 128
NEIGH = 2
S_DEV = 16
DB_DEV = 8
CAP = 4
SPANS = 256
TOKENS = 16384
NDB = 128
N_FSDP = 16
N_GRP = 8


def shared_layout(key):
    return jax.random.permutation(jax.random.fold_in(key, 7), NDB).astype(jnp.int32)


def draw_shard_map(key, part):
    return shared_layout(key)


def draw_neighbour_ids(key, part):
    layout = shared_layout(key)
    inverse = jnp.argsort(layout, stable=True).astype(jnp.int32)
    wanted = NEIGH * S_DEV
    hot_key = jax.random.fold_in(key, 13)
    hot_owner = jax.random.randint(hot_key, (), 0, N_FSDP).astype(jnp.int32)

    def one_block(block_key):
        split_keys = jax.random.split(block_key, 3)
        spare = jax.random.permutation(split_keys[0], (N_FSDP - 1) * CAP).astype(jnp.int32)[:wanted - CAP]
        other_owners = (hot_owner + 1 + spare // CAP) % N_FSDP
        owners = jnp.concatenate([jnp.full((CAP,), hot_owner, jnp.int32), other_owners.astype(jnp.int32)])
        owners = owners[jax.random.permutation(split_keys[1], wanted)]
        local_index = jax.random.randint(split_keys[2], (wanted,), 0, DB_DEV).astype(jnp.int32)
        return inverse[owners * DB_DEV + local_index]
    block_keys = jax.random.split(jax.random.fold_in(key, 11), N_FSDP)
    return jax.vmap(one_block)(block_keys).reshape(SPANS, NEIGH).astype(jnp.int32)


def steps_of(stream_key, shape, cuts, low, largest):
    def one(position, parts):
        steps = jax.random.uniform(jax.random.fold_in(jax.random.fold_in(stream_key, 6), position), (parts,), jnp.float32, low / len(cuts), largest / len(cuts))
        return jnp.repeat(jnp.exp(steps), shape[position] // parts).reshape((-1,) + (1,) * (len(shape) - position - 1))

    gain = one(*cuts[0])
    for cut in cuts[1:]:
        gain = gain * one(*cut)
    return gain


def bell_draw(rng, extent, spread, limit, shards=(), kind=jnp.bfloat16):
    gain = steps_of(rng, extent, shards, -0.22, 0.18) if shards else 1.0
    result = jax.random.normal(rng, extent, jnp.float32) * spread * gain
    return jnp.minimum(jnp.maximum(result, -limit), limit).astype(kind)


def setup_inputs(seed: int = 0) -> dict:
    key_list = jax.random.split(jax.random.key(seed), 9)
    tokens = bell_draw(key_list[0], (TOKENS, D), 1.0, 6.0, ((0, 16),))
    database = bell_draw(key_list[1], (NDB, NLEN, ENC), 1.0, 6.0, ((0, 16),))
    neighbour_ids = draw_neighbour_ids(jax.random.fold_in(key_list[8], 71), 0)
    shard_map = draw_shard_map(jax.random.fold_in(key_list[8], 71), 0)
    q_weight = bell_draw(key_list[4], (D, HEADS * HEAD), D ** -0.5, 0.09375, ((0, 16), (1, 8)))
    k_weight = bell_draw(key_list[5], (ENC, HEADS * HEAD), ENC ** -0.5, 0.1875, ((0, 16), (1, 8)))
    v_weight = bell_draw(key_list[6], (ENC, HEADS * HEAD), ENC ** -0.5, 0.1875, ((0, 16), (1, 8)))
    o_weight = bell_draw(key_list[7], (HEADS * HEAD, D), (D // 64) ** -0.5, 0.75, ((0, 8), (1, 16)))
    return {"tokens": tokens, "database": database, "neighbour_ids": neighbour_ids, "shard_map": shard_map, "q_weight": q_weight, "k_weight": k_weight, "v_weight": v_weight, "o_weight": o_weight}


norm_eps = 1e-06

def head_norm(field):
    shaped = field.reshape(field.shape[:-1] + (field.shape[-1] // HEAD, HEAD))
    scaled = shaped * lax.rsqrt(lax.optimization_barrier(jnp.mean(shaped * shaped, axis=-1, keepdims=True)) + norm_eps)
    return scaled.reshape(field.shape)

def reference(tokens, database, neighbour_ids, shard_map, q_weight, k_weight, v_weight, o_weight):
    queries = jnp.dot(tokens, q_weight, preferred_element_type=jnp.float32)
    query_hat = lax.optimization_barrier(head_norm(queries).astype(jnp.bfloat16))
    stored_at = jnp.take(shard_map, neighbour_ids, axis=0).astype(jnp.int32)
    query_blocks = query_hat.reshape(SPANS, SPAN, HEADS, HEAD)

    def one_span(inputs):
        query_block, where_rows = inputs
        rows = jnp.take(database, where_rows, axis=0).reshape(NEIGH * NLEN, ENC)
        key_hat = head_norm(jnp.dot(rows, k_weight, preferred_element_type=jnp.float32)).astype(jnp.bfloat16)
        key_hat = lax.optimization_barrier(key_hat)
        values = lax.optimization_barrier(jnp.dot(rows, v_weight, preferred_element_type=jnp.float32).astype(jnp.bfloat16))
        key_block = key_hat.astype(jnp.float32).reshape(NEIGH * NLEN, HEADS, HEAD)
        value_block = values.astype(jnp.float32).reshape(NEIGH * NLEN, HEADS, HEAD)
        scores = jnp.einsum('qhd,khd->hqk', query_block.astype(jnp.float32), key_block, precision=lax.Precision.HIGHEST) / math.sqrt(HEAD)
        raised = jnp.exp(scores)
        soft_weights = lax.optimization_barrier((raised / lax.optimization_barrier(jnp.sum(raised, axis=-1, keepdims=True))).astype(jnp.bfloat16))
        mixed_heads = jnp.einsum('hqk,khd->qhd', soft_weights.astype(jnp.float32), value_block, precision=lax.Precision.HIGHEST)
        return mixed_heads.astype(jnp.bfloat16)
    attended = lax.map(one_span, (query_blocks, stored_at)).reshape(TOKENS, HEADS * HEAD)
    group_width = HEADS * HEAD // N_GRP
    attended_groups = attended.reshape(TOKENS, N_GRP, group_width).transpose(1, 0, 2)
    weight_groups = o_weight.reshape(N_GRP, group_width, D)

    def add_group(total, pieces):
        group_rows, group_weight = pieces
        term = jnp.dot(group_rows, group_weight, preferred_element_type=jnp.float32).astype(jnp.bfloat16)
        term = lax.optimization_barrier(term)
        return (total + term.astype(jnp.float32), None)
    total, unused = lax.scan(add_group, jnp.zeros((TOKENS, D), jnp.float32), (attended_groups, weight_groups))
    return total.astype(jnp.bfloat16)
```

```python
import functools
import math

import jax
import jax.numpy as jnp
from jax import lax
from jax.experimental import pallas as pl
from jax.experimental.pallas import tpu as pltpu
from jax.sharding import PartitionSpec as P

HEAD = 128
EPS = 1e-06
RING = 4
ORDER = (0, 3, 1, 2)
PLACE = (0, 2, 3, 1)
VMEM_LIMIT = 56 * 1024 * 1024
ANY = pl.BlockSpec(memory_space=pl.ANY)
VMEM = pl.BlockSpec(memory_space=pltpu.VMEM)


def shift(value, axis, step):
    size = lax.axis_size(axis)
    return lax.ppermute(value, axis, [(i, (i + step) % size) for i in range(size)])


def gather_small(block, axis):
    return jnp.stack(
        [block, shift(block, axis, 1), shift(block, axis, -1), shift(block, axis, 2)]
    )


def gather_ring(blocks, axis):
    half = blocks.shape[0] // 2
    before, after = shift(blocks, axis, 1), shift(blocks, axis, -1)
    return [
        blocks,
        before,
        after,
        shift(before[:half], axis, 1),
        shift(after[half:], axis, -1),
    ]


def after(value, *earlier):
    return lax.optimization_barrier((value,) + earlier)[0]


BLOCKS = tuple((p, s) for p in range(3) for s in range(4)) + ((3, 0), (3, 1), (4, 0), (4, 1))


def block_owners(z, y):
    major = jnp.array([ORDER[k // 4] for k in range(16)], jnp.int32)
    minor = jnp.array([ORDER[k % 4] for k in range(16)], jnp.int32)
    by_zy = ((z + minor) % RING) * RING + (y + major) % RING
    by_yz = ((z + major) % RING) * RING + (y + minor) % RING
    return by_zy.astype(jnp.int32), by_yz.astype(jnp.int32)


def pick_kernel(place_ref, *refs):
    pieces, (out_ref, sem) = refs[:5], refs[5:]
    bounds = (0, 32, 64, 96, 112, 128)

    def one(j, carry):
        place = place_ref[j]
        for low, high, piece in zip(bounds[:-1], bounds[1:], pieces):

            @pl.when((place >= low) & (place < high))
            def _():
                pltpu.make_async_copy(piece.at[place - low], out_ref.at[j], sem).start()

        return carry

    lax.fori_loop(0, out_ref.shape[0], one, 0)
    pltpu.make_async_copy(out_ref, out_ref, sem).wait()


def pick(place, pieces, count):
    shape = pieces[0].shape[1:]
    return pl.pallas_call(
        pick_kernel,
        out_shape=jax.ShapeDtypeStruct((count,) + shape, jnp.bfloat16),
        grid_spec=pltpu.PrefetchScalarGridSpec(
            num_scalar_prefetch=1,
            grid=(1,),
            in_specs=[ANY] * 5,
            out_specs=VMEM,
            scratch_shapes=[pltpu.SemaphoreType.DMA],
        ),
        cost_estimate=pl.CostEstimate(flops=0, bytes_accessed=2 * 1024 * 1024, transcendentals=0),
        name="pick",
    )(place, *pieces)


def arrange_kernel(owner_ref, *refs):
    pieces, (out_ref, sem) = refs[:5], refs[5:]
    for k, (p, s) in enumerate(BLOCKS):
        pltpu.make_async_copy(pieces[p].at[s], out_ref.at[owner_ref[k]], sem).start()
    pltpu.make_async_copy(out_ref, out_ref, sem).wait()


def arrange(owners, pieces):
    return pl.pallas_call(
        arrange_kernel,
        out_shape=jax.ShapeDtypeStruct((16,) + pieces[0].shape[1:], jnp.bfloat16),
        grid_spec=pltpu.PrefetchScalarGridSpec(
            num_scalar_prefetch=1,
            grid=(1,),
            in_specs=[ANY] * 5,
            out_specs=VMEM,
            scratch_shapes=[pltpu.SemaphoreType.DMA],
        ),
        cost_estimate=pl.CostEstimate(flops=0, bytes_accessed=4 * 1024 * 1024, transcendentals=0),
        name="arrange",
    )(owners, *pieces)


def normed(field):
    parts = []
    for h in range(field.shape[1] // HEAD):
        part = field[:, h * HEAD : (h + 1) * HEAD]
        scale = lax.rsqrt(jnp.mean(part * part, axis=-1, keepdims=True) + EPS)
        parts.append((part * scale).astype(jnp.bfloat16))
    return parts


def query_kernel(owner_ref, tokens_ref, *refs):
    pieces, (out_ref, weight_ref, sem) = refs[:5], refs[5:]

    @pl.when(pl.program_id(0) == 0)
    def _():
        for k, (p, s) in enumerate(BLOCKS):
            rows = pl.multiple_of(owner_ref[k] * 256, 256)
            pltpu.make_async_copy(
                pieces[p].at[s], weight_ref.at[pl.ds(rows, 256), :], sem
            ).start()
        pltpu.make_async_copy(weight_ref, weight_ref, sem).wait()

    field = jnp.dot(tokens_ref[...], weight_ref[...], preferred_element_type=jnp.float32)
    for h, part in enumerate(normed(field)):
        out_ref[:, h * HEAD : (h + 1) * HEAD] = part


def query_projection(owners, tokens, pieces):
    rows, depth = tokens.shape
    width = pieces[0].shape[2]
    block = 256
    return pl.pallas_call(
        query_kernel,
        out_shape=jax.ShapeDtypeStruct((rows, width), jnp.bfloat16),
        grid_spec=pltpu.PrefetchScalarGridSpec(
            num_scalar_prefetch=1,
            grid=(rows // block,),
            in_specs=[pl.BlockSpec((block, depth), lambda i, s: (i, 0))] + [ANY] * 5,
            out_specs=pl.BlockSpec((block, width), lambda i, s: (i, 0)),
            scratch_shapes=[
                pltpu.VMEM((depth, width), jnp.bfloat16),
                pltpu.SemaphoreType.DMA,
            ],
        ),
        compiler_params=pltpu.CompilerParams(vmem_limit_bytes=VMEM_LIMIT),
        cost_estimate=pl.CostEstimate(
            flops=2 * rows * depth * width, bytes_accessed=14 * 1024 * 1024, transcendentals=0
        ),
        name="query_projection",
    )(owners, tokens, *pieces)


def rows_kernel(mine_ref, other_ref, panel_ref, k_ref, v_ref):
    near, share, depth = mine_ref.shape
    half = k_ref.shape[-1]
    rows = jnp.concatenate([mine_ref[...], other_ref[...]], axis=1)
    rows = rows.reshape(near * 2 * share, depth)
    keys = jnp.dot(rows, panel_ref[:, :half], preferred_element_type=jnp.float32)
    values = jnp.dot(rows, panel_ref[:, half:], preferred_element_type=jnp.float32)
    for h, part in enumerate(normed(keys)):
        k_ref[:, :, h * HEAD : (h + 1) * HEAD] = part.reshape(near, 2 * share, HEAD)
    v_ref[...] = values.astype(jnp.bfloat16).reshape(near, 2 * share, half)


def project_rows(mine, other, panel):
    near, share, depth = mine.shape
    width = panel.shape[1] // 2
    block = 8
    shape = jax.ShapeDtypeStruct((near, 2 * share, width), jnp.bfloat16)
    spec = pl.BlockSpec((block, share, depth), lambda i: (i, 0, 0))
    out_spec = pl.BlockSpec((block, 2 * share, width), lambda i: (i, 0, 0))
    return pl.pallas_call(
        rows_kernel,
        out_shape=(shape, shape),
        grid=(near // block,),
        in_specs=[spec, spec, VMEM],
        out_specs=(out_spec, out_spec),
        compiler_params=pltpu.CompilerParams(vmem_limit_bytes=VMEM_LIMIT),
        cost_estimate=pl.CostEstimate(
            flops=4 * near * 2 * share * depth * width,
            bytes_accessed=6 * 1024 * 1024,
            transcendentals=0,
        ),
        name="project_rows",
    )(mine, other, panel)


def attend_kernel(query_ref, *refs):
    k_refs, v_refs, out_ref = refs[:4], refs[4:8], refs[8]
    heads = out_ref.shape[1] // HEAD
    spans, span, near = out_ref.shape[0] // 64, 64, 2
    scale = math.log2(math.e) / math.sqrt(HEAD)

    def of_span(piece_refs, s, lanes):
        rows = [r[s * near : (s + 1) * near, :, lanes].reshape(-1, HEAD) for r in piece_refs]
        return jnp.concatenate(rows, axis=0)

    pairs = [(s, slice(h * HEAD, (h + 1) * HEAD)) for s in range(spans) for h in range(heads)]
    scores = [
        lax.dot_general(
            query_ref[s * span : (s + 1) * span, lanes],
            of_span(k_refs, s, lanes),
            (((1,), (1,)), ((), ())),
            preferred_element_type=jnp.float32,
        )
        for s, lanes in pairs
    ]
    raised = [jnp.exp2(score * scale) for score in scores]
    sums = [jnp.sum(r, axis=-1, keepdims=True) for r in raised]
    for (s, lanes), r, total in zip(pairs, raised, sums):
        mixed = jnp.dot(
            r.astype(jnp.bfloat16), of_span(v_refs, s, lanes), preferred_element_type=jnp.float32
        )
        out_ref[s * span : (s + 1) * span, lanes] = (mixed / total).astype(jnp.bfloat16)


def attend(query, keys, values):
    rows, width = query.shape
    spans = 2
    block = spans * 64
    near = spans * 2
    piece = keys[0].shape
    return pl.pallas_call(
        attend_kernel,
        out_shape=jax.ShapeDtypeStruct((rows, width), jnp.bfloat16),
        grid=(rows // block,),
        in_specs=[pl.BlockSpec((block, width), lambda i: (i, 0))]
        + [pl.BlockSpec((near,) + piece[1:], lambda i: (i, 0, 0))] * 8,
        out_specs=pl.BlockSpec((block, width), lambda i: (i, 0)),
        compiler_params=pltpu.CompilerParams(vmem_limit_bytes=VMEM_LIMIT),
        cost_estimate=pl.CostEstimate(
            flops=4_000_000_000, bytes_accessed=12 * 1024 * 1024, transcendentals=4_000_000
        ),
        name="attend",
    )(query, *keys, *values)


def mix_kernel(turn_ref, mine_ref, other_ref, *refs):
    mine_w, other_w, outs = refs[:5], refs[5:10], refs[10:]
    rows = mine_ref.shape[1]
    order = [turn_ref[k] for k in (2, 1, 3, 0)]
    mine = jnp.concatenate([mine_ref[t] for t in order], axis=0)
    other = jnp.concatenate([other_ref[t] for t in order], axis=0)
    for j, (p, s) in enumerate(BLOCKS):
        total = jnp.dot(mine, mine_w[p][s], preferred_element_type=jnp.float32)
        total += jnp.dot(other, other_w[p][s], preferred_element_type=jnp.float32)
        total = total.astype(jnp.bfloat16)
        at = j % 8 * 256
        for k in range(4):
            outs[k * 2 + j // 8][:, at : at + 256] = total[k * rows : (k + 1) * rows]


def mix(turn, mine, other, mine_w, other_w):
    shape = jax.ShapeDtypeStruct((128, 2048), jnp.bfloat16)
    return pl.pallas_call(
        mix_kernel,
        out_shape=[shape] * 8,
        grid_spec=pltpu.PrefetchScalarGridSpec(
            num_scalar_prefetch=1,
            grid=(1,),
            in_specs=[VMEM] * 12,
            out_specs=[VMEM] * 8,
        ),
        compiler_params=pltpu.CompilerParams(vmem_limit_bytes=VMEM_LIMIT),
        cost_estimate=pl.CostEstimate(
            flops=2 * 512 * 1024 * 4096, bytes_accessed=14 * 1024 * 1024, transcendentals=0
        ),
        name="mix",
    )(turn, mine, other, *mine_w, *other_w)


def final_kernel(owner_ref, *refs):
    ins, out_ref = refs[:6], refs[6]
    for j in range(16):
        lanes = slice(j % 8 * 256, (j % 8 + 1) * 256)
        total = sum(ins[j // 8 * 3 + i][:, lanes].astype(jnp.float32) for i in range(3))
        at = pl.multiple_of(owner_ref[j] * 256, 256)
        out_ref[:, pl.ds(at, 256)] = total.astype(jnp.bfloat16)


def final(owners, parts):
    return pl.pallas_call(
        final_kernel,
        out_shape=jax.ShapeDtypeStruct((128, 4096), jnp.bfloat16),
        grid_spec=pltpu.PrefetchScalarGridSpec(
            num_scalar_prefetch=1, grid=(1,), in_specs=[VMEM] * 6, out_specs=VMEM
        ),
        compiler_params=pltpu.CompilerParams(vmem_limit_bytes=VMEM_LIMIT),
        name="final",
    )(owners, *parts)


def added(a, b):
    return (a.astype(jnp.float32) + b.astype(jnp.float32)).astype(jnp.bfloat16)


def local(tokens, database, neighbour_ids, shard_map, q_weight, k_weight, v_weight, o_weight):
    z, y, x, core = (lax.axis_index(a) for a in ("z", "y", "x", "core"))
    by_zy, by_yz = block_owners(z, y)
    stored = database.shape[0]

    ids = neighbour_ids.reshape(-1)
    span_ids = jnp.arange(shard_map.shape[0], dtype=jnp.int32)
    at = jnp.sum(jnp.where(ids[:, None] == span_ids[None, :], shard_map[None, :], 0), axis=1)
    owner, index = at // stored, at % stored
    dz, dy = (owner // RING - z) % RING, (owner % RING - y) % RING
    place_of = lambda d: jnp.where(d == 0, 0, jnp.where(d == 3, 1, d + 1))
    place = ((place_of(dy) * RING + place_of(dz)) * stored + index).astype(jnp.int32)

    share = lax.dynamic_slice_in_dim(database, (x * 2 + core) * 16, 16, axis=1)
    near_z = gather_small(share, "z")
    kv_y = gather_small(jnp.concatenate([k_weight, v_weight], axis=1), "y")
    q_y = gather_small(q_weight, "y")
    all_rows = gather_ring(near_z, "y")
    kv_all = gather_ring(after(kv_y, near_z), "z")
    o_z = gather_small(after(o_weight, near_z), "z")
    q_all = gather_ring(after(q_y, o_z), "z")
    o_all = gather_ring(after(o_z, *all_rows), "y")

    flat = [p.reshape((-1,) + p.shape[2:]) for p in all_rows]
    wanted = pick(place, flat, ids.shape[0])

    ring = gather_ring(wanted, "x")
    rings = ring[:3] + [jnp.concatenate(ring[3:], axis=0)]
    others = [shift(r, "core", 1) for r in rings]

    blocks = arrange(by_yz, kv_all)
    panel = blocks.reshape(-1, blocks.shape[-1])
    keys, values = zip(*[project_rows(a, b, panel) for a, b in zip(rings, others)])
    query = query_projection(by_yz, tokens, q_all)
    attended = attend(query, keys, values)

    o_other = [shift(w, "core", 1) for w in o_all]
    by_core = attended.reshape(4, 2, 128, attended.shape[1])
    mine = lax.dynamic_index_in_dim(by_core, core, axis=1, keepdims=False)
    give = lax.dynamic_index_in_dim(by_core, 1 - core, axis=1, keepdims=False)
    other = shift(give, "core", 1)
    turn = ((x + jnp.arange(4)) % RING).astype(jnp.int32)
    t2a, t2b, t1a, t1b, t3a, t3b, t0a, t0b = mix(turn, mine, other, o_all, o_other)

    to_next, to_last = shift(t2a, "x", 1), shift(t2b, "x", -1)
    r1b, r3a = shift(t1b, "x", 1), shift(t3a, "x", -1)
    r1a = shift(added(t1a, to_next), "x", 1)
    r3b = shift(added(t3b, to_last), "x", -1)
    return final(by_zy, [t0a, r1a, r3a, t0b, r1b, r3b])


def solution(mesh):
    grid = jax.sharding.Mesh(mesh.devices.reshape(4, 4, 4, 2), ("z", "y", "x", "core"))
    fsdp, grp = ("z", "y"), ("x", "core")
    in_specs = (
        P(fsdp, None),
        P(fsdp, None, None),
        P(fsdp, None),
        P(),
        P(fsdp, grp),
        P(fsdp, grp),
        P(fsdp, grp),
        P(grp, fsdp),
    )
    out_specs = P(fsdp + grp, None)
    return jax.shard_map(local, mesh=grid, in_specs=in_specs, out_specs=out_specs, check_vma=False)
```

```python
import functools
import math

import jax
import jax.numpy as jnp
from jax import lax
from jax.experimental import pallas as pl
from jax.experimental.pallas import tpu as pltpu
from jax.sharding import PartitionSpec as P

HEAD = 128
EPS = 1e-06
RING = 4
ORDER = (0, 3, 1, 2)
PLACE = (0, 2, 3, 1)
MIB = 1024 * 1024
ANY = pl.BlockSpec(memory_space=pl.ANY)
VMEM = pl.BlockSpec(memory_space=pltpu.VMEM)


def shift(value, axis, step):
    size = lax.axis_size(axis)
    return lax.ppermute(value, axis, [(i, (i + step) % size) for i in range(size)])


def hold(values, *earlier):
    count = len(values)
    return list(lax.optimization_barrier(tuple(values) + earlier)[:count])


def line(block, axis):
    return [block, shift(block, axis, 1), shift(block, axis, -1), shift(block, axis, 2)]


def ring_near(blocks, axis):
    return [blocks, shift(blocks, axis, 1), shift(blocks, axis, -1)]


def after(value, *earlier):
    return hold([value], *earlier)[0]


def far_halves(pieces):
    _, before, behind = pieces
    half = before.shape[0] // 2
    return [before[:half], behind[half:]]


def ring_far(pieces, halves, axis):
    return pieces + [shift(halves[0], axis, 1), shift(halves[1], axis, -1)]


BLOCKS = tuple((p, s) for p in range(3) for s in range(4)) + ((3, 0), (3, 1), (4, 0), (4, 1))


def block_owners(z, y):
    major = jnp.array([ORDER[k // 4] for k in range(16)], jnp.int32)
    minor = jnp.array([ORDER[k % 4] for k in range(16)], jnp.int32)
    by_zy = ((z + minor) % RING) * RING + (y + major) % RING
    by_yz = ((z + major) % RING) * RING + (y + minor) % RING
    return by_zy.astype(jnp.int32), by_yz.astype(jnp.int32)


def pick_kernel(place_ref, *refs):
    pieces, (out_ref, sem) = refs[:10], refs[10:]
    bounds = (0, 16, 32, 48, 56, 64, 80, 96, 112, 120, 128)

    def one(j, carry):
        place = place_ref[j]
        for low, high, piece in zip(bounds[:-1], bounds[1:], pieces):

            @pl.when((place >= low) & (place < high))
            def _():
                pltpu.make_async_copy(piece.at[place - low], out_ref.at[j], sem).start()

        return carry

    lax.fori_loop(0, out_ref.shape[0], one, 0)
    pltpu.make_async_copy(out_ref, out_ref, sem).wait()


def pick(place, pieces, count):
    shape = pieces[0].shape[1:]
    return pl.pallas_call(
        pick_kernel,
        out_shape=jax.ShapeDtypeStruct((count,) + shape, jnp.bfloat16),
        grid_spec=pltpu.PrefetchScalarGridSpec(
            num_scalar_prefetch=1,
            grid=(1,),
            in_specs=[ANY] * 10,
            out_specs=VMEM,
            scratch_shapes=[pltpu.SemaphoreType.DMA],
        ),
        compiler_params=pltpu.CompilerParams(vmem_limit_bytes=8 * MIB),
        cost_estimate=pl.CostEstimate(flops=0, bytes_accessed=2 * MIB, transcendentals=0),
        name="pick",
    )(place, *pieces)


def arrange_kernel(owner_ref, *refs):
    pieces, (out_ref, sem) = refs[:5], refs[5:]
    for k, (p, s) in enumerate(BLOCKS):
        pltpu.make_async_copy(pieces[p].at[s], out_ref.at[owner_ref[k]], sem).start()
    pltpu.make_async_copy(out_ref, out_ref, sem).wait()


def arrange(owners, pieces):
    return pl.pallas_call(
        arrange_kernel,
        out_shape=jax.ShapeDtypeStruct((16,) + pieces[0].shape[1:], jnp.bfloat16),
        grid_spec=pltpu.PrefetchScalarGridSpec(
            num_scalar_prefetch=1,
            grid=(1,),
            in_specs=[ANY] * 5,
            out_specs=VMEM,
            scratch_shapes=[pltpu.SemaphoreType.DMA],
        ),
        compiler_params=pltpu.CompilerParams(vmem_limit_bytes=8 * MIB),
        cost_estimate=pl.CostEstimate(flops=0, bytes_accessed=4 * MIB, transcendentals=0),
        name="arrange",
    )(owners, *pieces)


def normed(field):
    parts = []
    for h in range(field.shape[1] // HEAD):
        part = field[:, h * HEAD : (h + 1) * HEAD]
        scale = lax.rsqrt(jnp.mean(part * part, axis=-1, keepdims=True) + EPS)
        parts.append((part * scale).astype(jnp.bfloat16))
    return parts


def query_kernel(owner_ref, tokens_ref, *refs):
    pieces, (out_ref, weight_ref, sem) = refs[:5], refs[5:]

    @pl.when(pl.program_id(0) == 0)
    def _():
        for k, (p, s) in enumerate(BLOCKS):
            rows = pl.multiple_of(owner_ref[k] * 256, 256)
            pltpu.make_async_copy(
                pieces[p].at[s], weight_ref.at[pl.ds(rows, 256), :], sem
            ).start()
        pltpu.make_async_copy(weight_ref, weight_ref, sem).wait()

    field = jnp.dot(tokens_ref[...], weight_ref[...], preferred_element_type=jnp.float32)
    for h, part in enumerate(normed(field)):
        out_ref[:, h * HEAD : (h + 1) * HEAD] = part


def query_projection(owners, tokens, pieces):
    rows, depth = tokens.shape
    width = pieces[0].shape[2]
    block = 256
    return pl.pallas_call(
        query_kernel,
        out_shape=jax.ShapeDtypeStruct((rows, width), jnp.bfloat16),
        grid_spec=pltpu.PrefetchScalarGridSpec(
            num_scalar_prefetch=1,
            grid=(rows // block,),
            in_specs=[pl.BlockSpec((block, depth), lambda i, s: (i, 0))] + [ANY] * 5,
            out_specs=pl.BlockSpec((block, width), lambda i, s: (i, 0)),
            scratch_shapes=[
                pltpu.VMEM((depth, width), jnp.bfloat16),
                pltpu.SemaphoreType.DMA,
            ],
        ),
        compiler_params=pltpu.CompilerParams(vmem_limit_bytes=20 * MIB),
        cost_estimate=pl.CostEstimate(
            flops=2 * rows * depth * width, bytes_accessed=14 * MIB, transcendentals=0
        ),
        name="query_projection",
    )(owners, tokens, *pieces)


def attend_kernel(block_ref, query_ref, panel_ref, *refs):
    row_refs, out_ref = refs[:10], refs[10]
    block = block_ref[pl.program_id(0)]
    half = panel_ref.shape[1] // 2
    heads = half // HEAD
    near, share, depth = row_refs[0].shape
    low, high = row_refs[3:5], row_refs[8:10]
    shares = [r[...] for r in row_refs[:3] + row_refs[5:8]]
    shares += [jnp.where(block < 4, pair[0][...], pair[1][...]) for pair in (low, high)]
    rows = jnp.concatenate(shares, axis=1).reshape(near * 8 * share, depth)
    keys = normed(jnp.dot(rows, panel_ref[:, :half], preferred_element_type=jnp.float32))
    values = jnp.dot(rows, panel_ref[:, half:], preferred_element_type=jnp.float32).astype(
        jnp.bfloat16
    )
    span, per = 64, near * 4 * share
    scale = math.log2(math.e) / math.sqrt(HEAD)
    pairs = [(s, h) for s in range(2) for h in range(heads)]
    scores = [
        lax.dot_general(
            query_ref[s * span : (s + 1) * span, h * HEAD : (h + 1) * HEAD],
            keys[h][s * per : (s + 1) * per],
            (((1,), (1,)), ((), ())),
            preferred_element_type=jnp.float32,
        )
        for s, h in pairs
    ]
    raised = [jnp.exp2(score * scale) for score in scores]
    sums = [jnp.sum(r, axis=-1, keepdims=True) for r in raised]
    for (s, h), r, total in zip(pairs, raised, sums):
        lanes = slice(h * HEAD, (h + 1) * HEAD)
        mixed = jnp.dot(
            r.astype(jnp.bfloat16),
            values[s * per : (s + 1) * per, lanes],
            preferred_element_type=jnp.float32,
        )
        out_ref[s * span : (s + 1) * span, lanes] = (mixed / total).astype(jnp.bfloat16)


def attend(blocks, query, panel, pieces):
    width = query.shape[1]
    count, block, near = blocks.shape[0], 128, 4
    shape = (near,) + pieces[0].shape[1:]
    spec = pl.BlockSpec(shape, lambda i, b: (b[i], 0, 0))
    low = pl.BlockSpec(shape, lambda i, b: (jnp.minimum(b[i], 3), 0, 0))
    high = pl.BlockSpec(shape, lambda i, b: (jnp.maximum(b[i] - 4, 0), 0, 0))
    return pl.pallas_call(
        attend_kernel,
        out_shape=jax.ShapeDtypeStruct((count * block, width), jnp.bfloat16),
        grid_spec=pltpu.PrefetchScalarGridSpec(
            num_scalar_prefetch=1,
            grid=(count,),
            in_specs=[pl.BlockSpec((block, width), lambda i, b: (b[i], 0)), VMEM]
            + [spec, spec, spec, low, high] * 2,
            out_specs=pl.BlockSpec((block, width), lambda i, b: (i, 0)),
        ),
        compiler_params=pltpu.CompilerParams(vmem_limit_bytes=24 * MIB),
        cost_estimate=pl.CostEstimate(
            flops=6_000_000_000, bytes_accessed=12 * MIB, transcendentals=2_000_000
        ),
        name="attend",
    )(blocks, query, panel, *pieces)


def mix_kernel(mine_ref, other_ref, *refs):
    mine_w, other_w, outs = refs[:5], refs[5:10], refs[10:]
    rows = mine_ref.shape[0] // 4
    for j, (p, s) in enumerate(BLOCKS):
        total = jnp.dot(mine_ref[...], mine_w[p][s], preferred_element_type=jnp.float32)
        total += jnp.dot(other_ref[...], other_w[p][s], preferred_element_type=jnp.float32)
        total = total.astype(jnp.bfloat16)
        at = j % 8 * 256
        for k in range(4):
            outs[k * 2 + j // 8][:, at : at + 256] = total[k * rows : (k + 1) * rows]


def mix(mine, other, mine_w, other_w):
    shape = jax.ShapeDtypeStruct((128, 2048), jnp.bfloat16)
    return pl.pallas_call(
        mix_kernel,
        out_shape=[shape] * 8,
        in_specs=[VMEM] * 12,
        out_specs=[VMEM] * 8,
        compiler_params=pltpu.CompilerParams(vmem_limit_bytes=24 * MIB),
        cost_estimate=pl.CostEstimate(
            flops=2 * 512 * 1024 * 4096, bytes_accessed=14 * MIB, transcendentals=0
        ),
        name="mix",
    )(mine, other, *mine_w, *other_w)


def final_kernel(owner_ref, *refs):
    ins, out_ref = refs[:6], refs[6]
    for j in range(16):
        lanes = slice(j % 8 * 256, (j % 8 + 1) * 256)
        total = sum(ins[j // 8 * 3 + i][:, lanes].astype(jnp.float32) for i in range(3))
        at = pl.multiple_of(owner_ref[j] * 256, 256)
        out_ref[:, pl.ds(at, 256)] = total.astype(jnp.bfloat16)


def final(owners, parts):
    return pl.pallas_call(
        final_kernel,
        out_shape=jax.ShapeDtypeStruct((128, 4096), jnp.bfloat16),
        grid_spec=pltpu.PrefetchScalarGridSpec(
            num_scalar_prefetch=1, grid=(1,), in_specs=[VMEM] * 6, out_specs=VMEM
        ),
        compiler_params=pltpu.CompilerParams(vmem_limit_bytes=20 * MIB),
        name="final",
    )(owners, *parts)


def added(a, b):
    return (a.astype(jnp.float32) + b.astype(jnp.float32)).astype(jnp.bfloat16)


def local(tokens, database, neighbour_ids, shard_map, q_weight, k_weight, v_weight, o_weight):
    z, y, x, core = (lax.axis_index(a) for a in ("z", "y", "x", "core"))
    by_zy, by_yz = block_owners(z, y)
    stored = database.shape[0]

    ids = neighbour_ids.reshape(-1)
    span_ids = jnp.arange(shard_map.shape[0], dtype=jnp.int32)
    at = jnp.sum(jnp.where(ids[:, None] == span_ids[None, :], shard_map[None, :], 0), axis=1)
    owner, index = at // stored, at % stored
    dz, dy = (owner // RING - z) % RING, (owner % RING - y) % RING
    place_of = lambda d: jnp.where(d == 0, 0, jnp.where(d == 3, 1, d + 1))
    second = index // RING
    place = 64 * second + index % RING
    place += jnp.where(
        second == 0,
        place_of(dy) * 16 + place_of(dz) * RING,
        place_of(dz) * 16 + place_of(dy) * RING,
    )
    place = place.astype(jnp.int32)

    share = lax.dynamic_slice_in_dim(database, (x * 2 + core) * 16, 16, axis=1)
    first_z, second_y = line(share[:RING], "z"), line(share[RING:], "y")
    first_all, second_all = hold([jnp.stack(first_z), jnp.stack(second_y)])
    first_near, second_near = ring_near(first_all, "y"), ring_near(second_all, "z")
    halves = hold(far_halves(first_near) + far_halves(second_near))
    first_far = ring_far(first_near, halves[:2], "y")
    second_far = ring_far(second_near, halves[2:], "z")

    kv_weight = jnp.concatenate([k_weight, v_weight], axis=1)
    q_weight, o_weight, kv_weight = hold([q_weight, o_weight, kv_weight], *halves)
    lines = line(q_weight, "y") + line(o_weight, "z") + line(kv_weight, "z")

    flat = [p.reshape((-1,) + p.shape[2:]) for p in first_far + second_far]
    wanted = pick(place, flat, ids.shape[0])
    near_x = ring_near(wanted, "x")
    lines = hold(lines, wanted)
    q_all, o_all, kv_all = (jnp.stack(lines[i : i + RING]) for i in (0, RING, 2 * RING))
    q_near, kv_near = ring_near(q_all, "z"), ring_near(kv_all, "y")
    halves = hold(far_halves(kv_near))
    kv_far = ring_far(kv_near, halves, "y")
    o_near = ring_near(hold([o_all], *halves)[0], "y")
    blocks = arrange(by_zy, kv_far)
    panel = blocks.reshape(-1, blocks.shape[-1])

    halves = hold(far_halves(near_x) + far_halves(q_near), panel)
    pieces = hold(ring_far(near_x, halves[:2], "x"), *halves)
    q_far = ring_far(q_near, halves[2:], "z")
    query = query_projection(by_yz, tokens, q_far)
    halves = hold(far_halves(o_near), query)
    o_all = ring_far(o_near, halves, "y")
    pieces = pieces[:3] + hold(pieces[3:], *halves)
    pieces += [shift(p, "core", 1) for p in pieces]
    chips = (x + jnp.array([2, 1, 3, 0], jnp.int32)) % RING
    give = attend((chips * 2 + 1 - core).astype(jnp.int32), query, panel, pieces)
    other = shift(give, "core", 1)
    o_other = [shift(w, "core", 1) for w in hold(o_all[:3], give)]
    mine = attend((chips * 2 + core).astype(jnp.int32), after(query, give), panel, pieces)
    o_other += [shift(w, "core", 1) for w in hold(o_all[3:], mine)]
    t2a, t2b, t1a, t1b, t3a, t3b, t0a, t0b = mix(mine, other, o_all, o_other)

    to_next, to_last = shift(t2a, "x", 1), shift(t2b, "x", -1)
    r1b, r3a = shift(t1b, "x", 1), shift(t3a, "x", -1)
    r1a = shift(added(t1a, to_next), "x", 1)
    r3b = shift(added(t3b, to_last), "x", -1)
    return final(by_zy, [t0a, r1a, r3a, t0b, r1b, r3b])


def solution(mesh):
    grid = jax.sharding.Mesh(mesh.devices.reshape(4, 4, 4, 2), ("z", "y", "x", "core"))
    fsdp, grp = ("z", "y"), ("x", "core")
    in_specs = (
        P(fsdp, None),
        P(fsdp, None, None),
        P(fsdp, None),
        P(),
        P(fsdp, grp),
        P(fsdp, grp),
        P(fsdp, grp),
        P(grp, fsdp),
    )
    out_specs = P(fsdp + grp, None)
    return jax.shard_map(local, mesh=grid, in_specs=in_specs, out_specs=out_specs, check_vma=False)
```

```python
import functools
import math

import jax
import jax.numpy as jnp
from jax import lax
from jax.experimental import pallas as pl
from jax.experimental.pallas import tpu as pltpu
from jax.sharding import PartitionSpec as P

HEAD = 128
EPS = 1e-06
RING = 4
ORDER = (0, 3, 1, 2)
PLACE = (0, 2, 3, 1)
MIB = 1024 * 1024
ANY = pl.BlockSpec(memory_space=pl.ANY)
VMEM = pl.BlockSpec(memory_space=pltpu.VMEM)


def shift(value, axis, step):
    size = lax.axis_size(axis)
    return lax.ppermute(value, axis, [(i, (i + step) % size) for i in range(size)])


def hold(values, *earlier):
    count = len(values)
    return list(lax.optimization_barrier(tuple(values) + earlier)[:count])


def line(block, axis):
    return [block, shift(block, axis, 1), shift(block, axis, -1), shift(block, axis, 2)]


def ring_near(blocks, axis):
    return [blocks, shift(blocks, axis, 1), shift(blocks, axis, -1)]


def after(value, *earlier):
    return hold([value], *earlier)[0]


def far_halves(pieces):
    _, before, behind = pieces
    half = before.shape[0] // 2
    return [before[:half], behind[half:]]


def ring_far(pieces, halves, axis):
    return pieces + [shift(halves[0], axis, 1), shift(halves[1], axis, -1)]


BLOCKS = tuple((p, s) for p in range(3) for s in range(4)) + ((3, 0), (3, 1), (4, 0), (4, 1))


def block_owners(z, y):
    major = jnp.array([ORDER[k // 4] for k in range(16)], jnp.int32)
    minor = jnp.array([ORDER[k % 4] for k in range(16)], jnp.int32)
    by_zy = ((z + minor) % RING) * RING + (y + major) % RING
    by_yz = ((z + major) % RING) * RING + (y + minor) % RING
    return by_zy.astype(jnp.int32), by_yz.astype(jnp.int32)


def pick_kernel(place_ref, *refs):
    pieces, (out_ref, sem) = refs[:10], refs[10:]
    bounds = (0, 16, 32, 48, 56, 64, 80, 96, 112, 120, 128)

    def one(j, carry):
        place = place_ref[j]
        for low, high, piece in zip(bounds[:-1], bounds[1:], pieces):

            @pl.when((place >= low) & (place < high))
            def _():
                pltpu.make_async_copy(piece.at[place - low], out_ref.at[j], sem).start()

        return carry

    lax.fori_loop(0, out_ref.shape[0], one, 0)
    pltpu.make_async_copy(out_ref, out_ref, sem).wait()


def pick(place, pieces, count):
    shape = pieces[0].shape[1:]
    return pl.pallas_call(
        pick_kernel,
        out_shape=jax.ShapeDtypeStruct((count,) + shape, jnp.bfloat16),
        grid_spec=pltpu.PrefetchScalarGridSpec(
            num_scalar_prefetch=1,
            grid=(1,),
            in_specs=[ANY] * 10,
            out_specs=VMEM,
            scratch_shapes=[pltpu.SemaphoreType.DMA],
        ),
        compiler_params=pltpu.CompilerParams(vmem_limit_bytes=8 * MIB),
        cost_estimate=pl.CostEstimate(flops=0, bytes_accessed=2 * MIB, transcendentals=0),
        name="pick",
    )(place, *pieces)


def arrange_kernel(owner_ref, *refs):
    pieces, (out_ref, sem) = refs[:5], refs[5:]
    for k, (p, s) in enumerate(BLOCKS):
        pltpu.make_async_copy(pieces[p].at[s], out_ref.at[owner_ref[k]], sem).start()
    pltpu.make_async_copy(out_ref, out_ref, sem).wait()


def arrange(owners, pieces):
    return pl.pallas_call(
        arrange_kernel,
        out_shape=jax.ShapeDtypeStruct((16,) + pieces[0].shape[1:], jnp.bfloat16),
        grid_spec=pltpu.PrefetchScalarGridSpec(
            num_scalar_prefetch=1,
            grid=(1,),
            in_specs=[ANY] * 5,
            out_specs=VMEM,
            scratch_shapes=[pltpu.SemaphoreType.DMA],
        ),
        compiler_params=pltpu.CompilerParams(vmem_limit_bytes=8 * MIB),
        cost_estimate=pl.CostEstimate(flops=0, bytes_accessed=4 * MIB, transcendentals=0),
        name="arrange",
    )(owners, *pieces)


def normed(field):
    parts = []
    for h in range(field.shape[1] // HEAD):
        part = field[:, h * HEAD : (h + 1) * HEAD]
        scale = lax.rsqrt(jnp.mean(part * part, axis=-1, keepdims=True) + EPS)
        parts.append((part * scale).astype(jnp.bfloat16))
    return parts


def query_kernel(owner_ref, tokens_ref, *refs):
    pieces, (out_ref, weight_ref, sem) = refs[:5], refs[5:]

    @pl.when(pl.program_id(0) == 0)
    def _():
        for k, (p, s) in enumerate(BLOCKS):
            rows = pl.multiple_of(owner_ref[k] * 256, 256)
            pltpu.make_async_copy(
                pieces[p].at[s], weight_ref.at[pl.ds(rows, 256), :], sem
            ).start()
        pltpu.make_async_copy(weight_ref, weight_ref, sem).wait()

    field = jnp.dot(tokens_ref[...], weight_ref[...], preferred_element_type=jnp.float32)
    for h, part in enumerate(normed(field)):
        out_ref[:, h * HEAD : (h + 1) * HEAD] = part


def query_projection(owners, tokens, pieces):
    rows, depth = tokens.shape
    width = pieces[0].shape[2]
    block = 256
    return pl.pallas_call(
        query_kernel,
        out_shape=jax.ShapeDtypeStruct((rows, width), jnp.bfloat16),
        grid_spec=pltpu.PrefetchScalarGridSpec(
            num_scalar_prefetch=1,
            grid=(rows // block,),
            in_specs=[pl.BlockSpec((block, depth), lambda i, s: (i, 0))] + [ANY] * 5,
            out_specs=pl.BlockSpec((block, width), lambda i, s: (i, 0)),
            scratch_shapes=[
                pltpu.VMEM((depth, width), jnp.bfloat16),
                pltpu.SemaphoreType.DMA,
            ],
        ),
        compiler_params=pltpu.CompilerParams(vmem_limit_bytes=20 * MIB),
        cost_estimate=pl.CostEstimate(
            flops=2 * rows * depth * width, bytes_accessed=14 * MIB, transcendentals=0
        ),
        name="query_projection",
    )(owners, tokens, *pieces)


def attend_kernel(block_ref, query_ref, panel_ref, *refs):
    row_refs, out_ref = refs[:10], refs[10]
    block = block_ref[pl.program_id(0)]
    half = panel_ref.shape[1] // 2
    heads = half // HEAD
    near, share, depth = row_refs[0].shape
    low, high = row_refs[3:5], row_refs[8:10]
    shares = [r[...] for r in row_refs[:3] + row_refs[5:8]]
    shares += [jnp.where(block < 4, pair[0][...], pair[1][...]) for pair in (low, high)]
    rows = jnp.concatenate(shares, axis=1).reshape(near * 8 * share, depth)
    keys = normed(jnp.dot(rows, panel_ref[:, :half], preferred_element_type=jnp.float32))
    values = jnp.dot(rows, panel_ref[:, half:], preferred_element_type=jnp.float32).astype(
        jnp.bfloat16
    )
    span, per = 64, near * 4 * share
    scale = math.log2(math.e) / math.sqrt(HEAD)
    pairs = [(s, h) for s in range(2) for h in range(heads)]
    scores = [
        lax.dot_general(
            query_ref[s * span : (s + 1) * span, h * HEAD : (h + 1) * HEAD],
            keys[h][s * per : (s + 1) * per],
            (((1,), (1,)), ((), ())),
            preferred_element_type=jnp.float32,
        )
        for s, h in pairs
    ]
    raised = [jnp.exp2(score * scale) for score in scores]
    sums = [jnp.sum(r, axis=-1, keepdims=True) for r in raised]
    for (s, h), r, total in zip(pairs, raised, sums):
        lanes = slice(h * HEAD, (h + 1) * HEAD)
        mixed = jnp.dot(
            r.astype(jnp.bfloat16),
            values[s * per : (s + 1) * per, lanes],
            preferred_element_type=jnp.float32,
        )
        out_ref[s * span : (s + 1) * span, lanes] = (mixed / total).astype(jnp.bfloat16)


def attend(blocks, query, panel, pieces):
    width = query.shape[1]
    count, block, near = blocks.shape[0], 128, 4
    shape = (near,) + pieces[0].shape[1:]
    spec = pl.BlockSpec(shape, lambda i, b: (b[i], 0, 0))
    low = pl.BlockSpec(shape, lambda i, b: (jnp.minimum(b[i], 3), 0, 0))
    high = pl.BlockSpec(shape, lambda i, b: (jnp.maximum(b[i] - 4, 0), 0, 0))
    return pl.pallas_call(
        attend_kernel,
        out_shape=jax.ShapeDtypeStruct((count * block, width), jnp.bfloat16),
        grid_spec=pltpu.PrefetchScalarGridSpec(
            num_scalar_prefetch=1,
            grid=(count,),
            in_specs=[pl.BlockSpec((block, width), lambda i, b: (b[i], 0)), VMEM]
            + [spec, spec, spec, low, high] * 2,
            out_specs=pl.BlockSpec((block, width), lambda i, b: (i, 0)),
        ),
        compiler_params=pltpu.CompilerParams(vmem_limit_bytes=24 * MIB),
        cost_estimate=pl.CostEstimate(
            flops=6_000_000_000, bytes_accessed=12 * MIB, transcendentals=2_000_000
        ),
        name="attend",
    )(blocks, query, panel, *pieces)


def mix_kernel(mine_ref, other_ref, *refs):
    outs = refs[-4:]
    count = (len(refs) - 4) // 2
    rows = mine_ref.shape[0] // 4
    at = 0
    for mine_w, other_w in zip(refs[:count], refs[count:-4]):
        for s in range(mine_w.shape[0]):
            total = jnp.dot(mine_ref[...], mine_w[s], preferred_element_type=jnp.float32)
            total += jnp.dot(other_ref[...], other_w[s], preferred_element_type=jnp.float32)
            total = total.astype(jnp.bfloat16)
            for k in range(4):
                outs[k][:, at : at + 256] = total[k * rows : (k + 1) * rows]
            at += 256


def mix(mine, other, mine_w, other_w):
    shape = jax.ShapeDtypeStruct((128, 2048), jnp.bfloat16)
    return pl.pallas_call(
        mix_kernel,
        out_shape=[shape] * 4,
        in_specs=[VMEM] * (2 + 2 * len(mine_w)),
        out_specs=[VMEM] * 4,
        compiler_params=pltpu.CompilerParams(vmem_limit_bytes=16 * MIB),
        cost_estimate=pl.CostEstimate(
            flops=2 * 512 * 1024 * 2048, bytes_accessed=7 * MIB, transcendentals=0
        ),
        name="mix",
    )(mine, other, *mine_w, *other_w)


def final_kernel(owner_ref, *refs):
    ins, out_ref = refs[:6], refs[6]
    for j in range(16):
        lanes = slice(j % 8 * 256, (j % 8 + 1) * 256)
        total = sum(ins[j // 8 * 3 + i][:, lanes].astype(jnp.float32) for i in range(3))
        at = pl.multiple_of(owner_ref[j] * 256, 256)
        out_ref[:, pl.ds(at, 256)] = total.astype(jnp.bfloat16)


def final(owners, parts):
    return pl.pallas_call(
        final_kernel,
        out_shape=jax.ShapeDtypeStruct((128, 4096), jnp.bfloat16),
        grid_spec=pltpu.PrefetchScalarGridSpec(
            num_scalar_prefetch=1, grid=(1,), in_specs=[VMEM] * 6, out_specs=VMEM
        ),
        compiler_params=pltpu.CompilerParams(vmem_limit_bytes=20 * MIB),
        name="final",
    )(owners, *parts)


def added(a, b):
    return (a.astype(jnp.float32) + b.astype(jnp.float32)).astype(jnp.bfloat16)


def local(tokens, database, neighbour_ids, shard_map, q_weight, k_weight, v_weight, o_weight):
    z, y, x, core = (lax.axis_index(a) for a in ("z", "y", "x", "core"))
    by_zy, by_yz = block_owners(z, y)
    stored = database.shape[0]

    ids = neighbour_ids.reshape(-1)
    span_ids = jnp.arange(shard_map.shape[0], dtype=jnp.int32)
    at = jnp.sum(jnp.where(ids[:, None] == span_ids[None, :], shard_map[None, :], 0), axis=1)
    owner, index = at // stored, at % stored
    dz, dy = (owner // RING - z) % RING, (owner % RING - y) % RING
    place_of = lambda d: jnp.where(d == 0, 0, jnp.where(d == 3, 1, d + 1))
    second = index // RING
    place = 64 * second + index % RING
    place += jnp.where(
        second == 0,
        place_of(dy) * 16 + place_of(dz) * RING,
        place_of(dz) * 16 + place_of(dy) * RING,
    )
    place = place.astype(jnp.int32)

    share = lax.dynamic_slice_in_dim(database, (x * 2 + core) * 16, 16, axis=1)
    first_z, second_y = line(share[:RING], "z"), line(share[RING:], "y")
    first_all, second_all = hold([jnp.stack(first_z), jnp.stack(second_y)])
    first_near, second_near = ring_near(first_all, "y"), ring_near(second_all, "z")
    halves = hold(far_halves(first_near) + far_halves(second_near))
    first_far = ring_far(first_near, halves[:2], "y")
    second_far = ring_far(second_near, halves[2:], "z")

    kv_weight = jnp.concatenate([k_weight, v_weight], axis=1)
    q_weight, o_weight, kv_weight = hold([q_weight, o_weight, kv_weight], *halves)
    lines = line(q_weight, "y") + line(o_weight, "z") + line(kv_weight, "z")

    flat = [p.reshape((-1,) + p.shape[2:]) for p in first_far + second_far]
    wanted = pick(place, flat, ids.shape[0])
    near_x = ring_near(wanted, "x")
    lines = hold(lines, wanted)
    q_all, o_all, kv_all = (jnp.stack(lines[i : i + RING]) for i in (0, RING, 2 * RING))
    q_near, kv_near = ring_near(q_all, "z"), ring_near(kv_all, "y")
    halves = hold(far_halves(kv_near))
    kv_far = ring_far(kv_near, halves, "y")
    o_near = ring_near(hold([o_all], *halves)[0], "y")
    blocks = arrange(by_zy, kv_far)
    panel = blocks.reshape(-1, blocks.shape[-1])

    halves = hold(far_halves(near_x) + far_halves(q_near), panel)
    pieces = hold(ring_far(near_x, halves[:2], "x"), *halves)
    q_far = ring_far(q_near, halves[2:], "z")
    query = query_projection(by_yz, tokens, hold(q_far, *pieces[3:]))
    halves = hold(far_halves(o_near), *pieces[3:])
    o_all = ring_far(o_near, halves, "y")
    pieces = pieces[:3] + hold(pieces[3:], *halves)
    pieces += [shift(p, "core", 1) for p in pieces]
    chips = (x + jnp.array([2, 1, 3, 0], jnp.int32)) % RING
    give = attend((chips * 2 + 1 - core).astype(jnp.int32), query, panel, pieces)
    other = shift(give, "core", 1)
    o_other = [shift(w, "core", 1) for w in hold(o_all, give)]
    late = after(query, give, *o_all[3:])
    mine = attend((chips * 2 + core).astype(jnp.int32), late, panel, pieces)
    t2a, t1a, t3a, t0a = mix(mine, other, o_all[:2], o_other[:2])
    to_next, r3a = shift(t2a, "x", 1), shift(t3a, "x", -1)
    t2b, t1b, t3b, t0b = mix(after(mine, t2a), other, o_all[2:], o_other[2:])
    to_last, r1b = shift(t2b, "x", -1), shift(t1b, "x", 1)
    r1a = shift(added(t1a, to_next), "x", 1)
    r3b = shift(added(t3b, to_last), "x", -1)
    return final(by_zy, [t0a, r1a, r3a, t0b, r1b, r3b])


def solution(mesh):
    grid = jax.sharding.Mesh(mesh.devices.reshape(4, 4, 4, 2), ("z", "y", "x", "core"))
    fsdp, grp = ("z", "y"), ("x", "core")
    in_specs = (
        P(fsdp, None),
        P(fsdp, None, None),
        P(fsdp, None),
        P(),
        P(fsdp, grp),
        P(fsdp, grp),
        P(fsdp, grp),
        P(grp, fsdp),
    )
    out_specs = P(fsdp + grp, None)
    return jax.shard_map(local, mesh=grid, in_specs=in_specs, out_specs=out_specs, check_vma=False)
```
